512 devices in a mesh: samp: 64 (over y_lo, z, core), snp: 8 (over x, y_hi).
Axes of the slice: x: 4, y: 4 (y_hi: 2, y_lo: 2; y = y_hi * 2 + y_lo), z: 16, core: 2. Of those that a mesh axis runs over, the one named last changes fastest.
Arguments:
- genotype: int32 [65536, 4096], P('samp', 'snp'), may hold values from 0 to 3, as said below
- basis: bfloat16 [4096, 40], P('snp'), may hold values from -6 to 6
Outputs:
- sample_scores: bfloat16 [65536, 40], P('samp')
- snp_block: float32 [4096, 40], P('snp')
The draws below stay inside these ranges and needn't reach their ends.
Inputs may be any that keep to these rules, and one draw needn't show every extreme that they name: `genotype`: the value 3 marks a missing call; 0, 1 and 2 are dosages.
All inputs are finite; a program needn't handle non-finite values.
Results may differ from the reference program's by a relative error of at most 0.0065.
Values may be sent and summed in bfloat16 or wider, within the bound.
No kernel may reach another device: no remote copies, remote signals or barrier semaphores. Data moves between devices by JAX's collectives and lax.ppermute only.
A program may use at most 64 MiB of HBM per device.

```python
import jax
import jax.numpy as jnp
from jax import lax

M = 4096
K = 40
ITERS = 2
NS = 65536


def draw_genotype(key, part):
    key_base = jax.random.fold_in(key, 11)
    key_factor = jax.random.fold_in(key, 15)
    key_member = jax.random.fold_in(key, 16)
    key_first = jax.random.fold_in(key, 12)
    key_second = jax.random.fold_in(key, 13)
    key_missing = jax.random.fold_in(key, 14)
    base = jax.random.randint(key_base, (M,), 50, 300)
    cluster_factor = jax.random.randint(key_factor, (48, M), 250, 1750)
    table = base[None, :] * cluster_factor // 1000
    member = jax.random.randint(key_member, (NS,), 0, 48)
    thresh = table[member]
    first = jax.random.randint(key_first, (NS, M), 0, 1000)
    second = jax.random.randint(key_second, (NS, M), 0, 1000)
    dosage = (first < thresh).astype(jnp.int32) + (second < thresh).astype(jnp.int32)
    position = jnp.arange(NS, dtype=jnp.int32)
    keep_level = 300 + 600 * position // NS
    missing = jax.random.randint(key_missing, (NS, M), 0, 1000) >= keep_level[:, None]
    return jnp.where(missing, 3, dosage).astype(jnp.int32)


def level_of(key, dims, split, least, high):
    loudness, own = 1.0, jax.random.fold_in(key, 6)
    for axis_at, shards_of in split:
        steps = jnp.exp(jax.random.uniform(jax.random.fold_in(own, axis_at), (shards_of,), jnp.float32, least / len(split), high / len(split)))
        loudness = loudness * jnp.repeat(steps, dims[axis_at] // shards_of).reshape([-1 if axis == axis_at else 1 for axis in range(len(dims))])
    return loudness


def scatter_about(own_key, dims, scale, reach, cuts=(), kind=jnp.bfloat16):
    loudness = level_of(own_key, dims, cuts, -0.22, 0.18) if cuts else 1.0
    values = jax.random.normal(own_key, dims, jnp.float32) * scale * loudness
    return jnp.minimum(jnp.maximum(values, -reach), reach).astype(kind)


def setup_inputs(seed: int = 0) -> dict:
    key_of = jax.random.split(jax.random.key(seed), 3)
    return {
        "genotype": draw_genotype(jax.random.fold_in(key_of[2], 71), 0),
        "basis": scatter_about(key_of[1], (M, K), 1.0, 6.0, ((0, 8),)),
    }


def reference(genotype, basis):
    observed = genotype < 3
    dosage = jnp.where(observed, genotype, 0).astype(jnp.float32)
    allele_sum = lax.optimization_barrier(jnp.sum(dosage, axis=0))
    called = lax.optimization_barrier(jnp.sum(observed.astype(jnp.float32), axis=0))
    freq = (allele_sum + 1.0) / (2.0 * called + 2.0)
    scale = 1.0 / jnp.sqrt(2.0 * freq * (1.0 - freq))
    standard = jnp.where(observed, (dosage - 2.0 * freq) * scale, 0.0).astype(jnp.bfloat16)
    block = basis
    for step in range(ITERS):
        scores = jnp.dot(standard, block, preferred_element_type=jnp.float32)
        sample_scores = scores.astype(jnp.bfloat16)
        snp_block = jnp.dot(standard.T, sample_scores, preferred_element_type=jnp.float32) / NS
        block = snp_block.astype(jnp.bfloat16)
    return (sample_scores, snp_block)
```

```python
import jax
import jax.numpy as jnp
from jax import lax
from jax.sharding import PartitionSpec as P

ITERS = 2
LANES = 128


def samp_groups(mesh):
    size = mesh.shape["samp"]
    depth = size // 4
    at = lambda y, z, c: (y * depth + z) * 2 + c
    level = [[at(y, z, c) for y in range(2) for c in range(2)] for z in range(depth)]
    column = [[at(y, z, c) for z in range(depth)] for y in range(2) for c in range(2)]
    return level, column


def exchange(blocks, axis, groups=None):
    return lax.all_to_all(
        blocks, axis, split_axis=0, concat_axis=0, tiled=True, axis_index_groups=groups
    )


def from_all(shard, axis, members, groups=None):
    return exchange(jnp.broadcast_to(shard, (members, *shard.shape)), axis, groups)


def solution(mesh):
    level, column = samp_groups(mesh)
    near, far = len(level[0]), len(column[0])
    peers = mesh.shape["snp"]

    def over_samples(counts):
        held = from_all(counts.astype(jnp.int16), "samp", near, level)
        part = jnp.sum(held.astype(jnp.int32), axis=0)
        held = from_all(part.astype(jnp.int16), "samp", far, column)
        return jnp.sum(held.astype(jnp.int32), axis=0)

    def block_over_samples(local):
        rows, width = local.shape
        cut = local.astype(jnp.bfloat16).reshape(rows, near, width // near)
        arrived = exchange(cut.transpose(1, 0, 2), "samp", level)
        part = jnp.sum(arrived.astype(jnp.float32), axis=0).astype(jnp.bfloat16)
        held = from_all(part, "samp", far, column)
        share = jnp.sum(held.astype(jnp.float32), axis=0).astype(jnp.bfloat16)
        whole = from_all(share, "samp", near, level)
        return whole.transpose(1, 0, 2).reshape(rows, width)

    def per_device(genotype, basis):
        samples, snps = genotype.shape
        total = samples * lax.axis_size("samp")
        observed = genotype < 3
        dosage = jnp.where(observed, genotype, 0)
        counts = jnp.stack([jnp.sum(dosage, axis=0), jnp.sum(observed.astype(jnp.int32), axis=0)])
        counts = over_samples(counts.reshape(-1, LANES)).reshape(2, snps).astype(jnp.float32)
        freq = (counts[0] + 1.0) / (2.0 * counts[1] + 2.0)
        scale = 1.0 / jnp.sqrt(2.0 * freq * (1.0 - freq))
        standard = jnp.where(
            observed, (dosage.astype(jnp.float32) - 2.0 * freq) * scale, 0.0
        ).astype(jnp.bfloat16)
        block = basis.T
        for step in range(ITERS):
            part = lax.dot_general(
                block, standard, (((1,), (1,)), ((), ())), preferred_element_type=jnp.float32
            ).astype(jnp.bfloat16)
            held = from_all(part, "snp", peers)
            scores = jnp.sum(held.astype(jnp.float32), axis=0).astype(jnp.bfloat16)
            local = jnp.dot(scores, standard, preferred_element_type=jnp.float32)
            snp_block = block_over_samples(local).astype(jnp.float32) / total
            block = snp_block.astype(jnp.bfloat16)
        return scores.T, snp_block.T

    return jax.shard_map(
        per_device,
        mesh=mesh,
        in_specs=(P("samp", "snp"), P("snp", None)),
        out_specs=(P("samp", None), P("snp", None)),
        check_vma=False,
    )
```

```python
import jax
import jax.numpy as jnp
from jax import lax
from jax.sharding import PartitionSpec as P

ITERS = 2
LANES = 128
SUBLANES = 8
HALF = 16


def samp_groups(mesh):
    depth = mesh.shape["samp"] // 4
    at = lambda y, z, c: (y * depth + z) * 2 + c
    four = [(y, c) for y in range(2) for c in range(2)]
    level = [[at(y, z, c) for y, c in four] for z in range(depth)]
    column = [[at(y, z, c) for z in range(depth)] for y, c in four]
    cell = [[at(y, z + k, c) for k in range(2) for y, c in four] for z in range(0, depth, 2)]
    stride = [[at(y, z, c) for z in range(k, depth, 2)] for k in range(2) for y, c in four]
    return level, column, cell, stride


def exchange(blocks, axis, groups):
    return lax.all_to_all(
        blocks, axis, split_axis=0, concat_axis=0, tiled=True, axis_index_groups=groups
    )


def from_all(shard, axis, groups):
    copies = jnp.broadcast_to(shard, (len(groups[0]), *shard.shape))
    return exchange(copies, axis, groups)


def total_of(held):
    return jnp.sum(held.astype(jnp.float32), axis=0).astype(jnp.bfloat16)


def solution(mesh):
    level, column, cell, stride = samp_groups(mesh)
    peers = mesh.shape["snp"]
    snake = [[*range(0, peers, 2), *range(peers - 1, 0, -2)]]

    def block_over_samples(local):
        rows, width = local.shape
        members, tiles = len(cell[0]), width // LANES
        used = rows // SUBLANES * tiles
        each = -(-used // members)
        cut = local.astype(jnp.bfloat16).reshape(-1, SUBLANES, tiles, LANES)
        cut = cut.transpose(0, 2, 1, 3).reshape(used, SUBLANES, LANES)
        cut = jnp.pad(cut, ((0, each * members - used), (0, 0), (0, 0)))
        part = total_of(exchange(cut.reshape(members, each, SUBLANES, LANES), "samp", cell))
        share = total_of(from_all(part, "samp", stride))
        whole = from_all(share, "samp", cell).reshape(-1, SUBLANES, LANES)[:used]
        whole = whole.reshape(-1, tiles, SUBLANES, LANES).transpose(0, 2, 1, 3)
        return whole.reshape(rows, width)

    def per_device(genotype, basis):
        samples, snps = genotype.shape
        total = samples * lax.axis_size("samp")
        observed = genotype < 3
        counts = jnp.sum(jnp.where(observed, genotype + (1 << HALF), 0), axis=0)
        counts = jnp.sum(from_all(counts.reshape(-1, LANES), "samp", level), axis=0)
        held = from_all(counts, "samp", column)
        allele_sum = jnp.sum(held & ((1 << HALF) - 1), axis=0).astype(jnp.float32)
        called = jnp.sum(held >> HALF, axis=0).astype(jnp.float32)
        freq = (allele_sum + 1.0) / (2.0 * called + 2.0)
        scale = 1.0 / jnp.sqrt(2.0 * freq * (1.0 - freq))
        freq, scale = freq.reshape(snps), scale.reshape(snps)
        standard = jnp.where(
            observed, (genotype.astype(jnp.float32) - 2.0 * freq) * scale, 0.0
        ).astype(jnp.bfloat16)
        block = basis.T
        for step in range(ITERS):
            part = lax.dot_general(
                block, standard, (((1,), (1,)), ((), ())), preferred_element_type=jnp.float32
            ).astype(jnp.bfloat16)
            scores = total_of(from_all(part, "snp", snake))
            local = jnp.dot(scores, standard, preferred_element_type=jnp.float32)
            snp_block = block_over_samples(local).astype(jnp.float32) / total
            block = snp_block.astype(jnp.bfloat16)
        return scores.T, snp_block.T

    return jax.shard_map(
        per_device,
        mesh=mesh,
        in_specs=(P("samp", "snp"), P("snp", None)),
        out_specs=(P("samp", None), P("snp", None)),
        check_vma=False,
    )
```

```python
import jax
import jax.numpy as jnp
from jax import lax
from jax.sharding import PartitionSpec as P

ITERS = 2
LANES = 128
SUBLANES = 8
HALF = 16


def samp_groups(mesh):
    depth = mesh.shape["samp"] // 4
    at = lambda y, z, c: (y * depth + z) * 2 + c
    four = [(y, c) for y in range(2) for c in range(2)]
    zigzag = [k // 2 if k % 2 == 0 else depth - 1 - k // 2 for k in range(depth)]
    chip = [[at(y, z, c) for c in range(2)] for z in range(depth) for y in range(2)]
    side = [[at(y, z, c) for y in range(2)] for z in range(depth) for c in range(2)]
    level = [[at(y, z, c) for y, c in four] for z in range(depth)]
    column = [[at(y, z, c) for z in zigzag] for y, c in four]
    return chip, side, level, column


def exchange(blocks, axis, groups):
    return lax.all_to_all(
        blocks, axis, split_axis=0, concat_axis=0, tiled=True, axis_index_groups=groups
    )


def from_all(shard, axis, groups):
    copies = jnp.broadcast_to(shard, (len(groups[0]), *shard.shape))
    return exchange(copies, axis, groups)


def gather(shard, axis, groups):
    return lax.all_gather(shard, axis, axis_index_groups=groups)


def total_of(held):
    return jnp.sum(held.astype(jnp.float32), axis=0).astype(jnp.bfloat16)


def solution(mesh):
    chip, side, level, column = samp_groups(mesh)
    peers = mesh.shape["snp"]
    snake = [[*range(0, peers, 2), *range(peers - 1, 0, -2)]]

    def block_over_samples(local, y, core):
        rows, width = local.shape
        tiles = width // LANES
        cut = local.astype(jnp.bfloat16).reshape(-1, SUBLANES, tiles, LANES).transpose(0, 2, 1, 3)
        cut = cut.reshape(2, 2, -1, SUBLANES, LANES)
        half = total_of(lax.dynamic_index_in_dim(gather(cut, "samp", chip), core, 2, False))
        part = total_of(lax.dynamic_index_in_dim(gather(half, "samp", side), y, 1, False))
        share = total_of(from_all(part, "samp", column))
        whole = gather(share, "samp", level)
        whole = whole.reshape(-1, tiles, SUBLANES, LANES).transpose(0, 2, 1, 3)
        return whole.reshape(rows, width)

    def per_device(genotype, basis):
        samples, snps = genotype.shape
        total = samples * lax.axis_size("samp")
        at = lax.axis_index("samp").astype(jnp.uint32)
        y, core = (at >= lax.axis_size("samp") // 2).astype(jnp.uint32), at & 1
        observed = genotype < 3
        counts = jnp.sum(jnp.where(observed, genotype + (1 << HALF), 0), axis=0)
        counts, y, core = lax.optimization_barrier((counts, y, core))
        counts = jnp.sum(gather(counts.reshape(-1, LANES), "samp", level), axis=0)
        held = from_all(counts, "samp", column)
        allele_sum = jnp.sum(held & ((1 << HALF) - 1), axis=0).astype(jnp.float32)
        called = jnp.sum(held >> HALF, axis=0).astype(jnp.float32)
        freq = (allele_sum + 1.0) / (2.0 * called + 2.0)
        scale = 1.0 / jnp.sqrt(2.0 * freq * (1.0 - freq))
        freq, scale = freq.reshape(snps), scale.reshape(snps)
        standard = jnp.where(
            observed, (genotype.astype(jnp.float32) - 2.0 * freq) * scale, 0.0
        ).astype(jnp.bfloat16)
        block = basis.T
        for step in range(ITERS):
            part = lax.dot_general(
                block, standard, (((1,), (1,)), ((), ())), preferred_element_type=jnp.float32
            ).astype(jnp.bfloat16)
            scores = total_of(from_all(part, "snp", snake))
            local = jnp.dot(scores, standard, preferred_element_type=jnp.float32)
            snp_block = block_over_samples(local, y, core).astype(jnp.float32) / total
            block = snp_block.astype(jnp.bfloat16)
        return scores.T, snp_block.T

    return jax.shard_map(
        per_device,
        mesh=mesh,
        in_specs=(P("samp", "snp"), P("snp", None)),
        out_specs=(P("samp", None), P("snp", None)),
        check_vma=False,
    )
```

```python
import jax
import jax.numpy as jnp
from jax import lax
from jax.sharding import PartitionSpec as P

ITERS = 2
LANES = 128
SUBLANES = 8
HALF = 16


def samp_groups(mesh):
    depth = mesh.shape["samp"] // 4
    at = lambda y, z, c: (y * depth + z) * 2 + c
    four = [(y, c) for y in range(2) for c in range(2)]
    level = [[at(y, z, c) for y, c in four] for z in range(depth)]
    column = [[at(y, z, c) for z in range(depth)] for y, c in four]
    cell = [[at(y, z + k, c) for k in range(2) for y, c in four] for z in range(0, depth, 2)]
    stride = [[at(y, z, c) for z in range(k, depth, 2)] for k in range(2) for y, c in four]
    return level, column, cell, stride


def exchange(blocks, axis, groups):
    return lax.all_to_all(
        blocks, axis, split_axis=0, concat_axis=0, tiled=True, axis_index_groups=groups
    )


def from_all(shard, axis, groups):
    copies = jnp.broadcast_to(shard, (len(groups[0]), *shard.shape))
    return exchange(copies, axis, groups)


def total_of(held):
    return jnp.sum(held.astype(jnp.float32), axis=0)


def solution(mesh):
    level, column, cell, stride = samp_groups(mesh)
    peers = mesh.shape["snp"]
    snake = [[*range(0, peers, 2), *range(peers - 1, 0, -2)]]

    def block_over_samples(local, total, dtype):
        rows, width = local.shape
        members, tiles = len(cell[0]), width // LANES
        cut = local.astype(jnp.bfloat16).reshape(-1, SUBLANES, tiles, LANES)
        cut = cut.transpose(0, 2, 1, 3).reshape(members, -1, SUBLANES // 2, LANES)
        part = total_of(exchange(cut, "samp", cell)).astype(jnp.bfloat16)
        share = (total_of(from_all(part, "samp", stride)) / total).astype(dtype)
        whole = from_all(share, "samp", cell).reshape(-1, tiles, SUBLANES, LANES)
        return whole.transpose(0, 2, 1, 3).reshape(rows, width)

    def per_device(genotype, basis):
        samples, snps = genotype.shape
        total = samples * lax.axis_size("samp")
        observed = genotype < 3
        counts = jnp.sum(jnp.where(observed, genotype + (1 << HALF), 0), axis=0)
        counts = jnp.sum(from_all(counts.reshape(-1, LANES), "samp", level), axis=0)
        held = from_all(counts, "samp", column)
        allele_sum = jnp.sum(held & ((1 << HALF) - 1), axis=0).astype(jnp.float32)
        called = jnp.sum(held >> HALF, axis=0).astype(jnp.float32)
        freq = (allele_sum + 1.0) / (2.0 * called + 2.0)
        scale = 1.0 / jnp.sqrt(2.0 * freq * (1.0 - freq))
        freq, scale = freq.reshape(snps), scale.reshape(snps)
        standard = jnp.where(
            observed, (genotype.astype(jnp.float32) - 2.0 * freq) * scale, 0.0
        ).astype(jnp.bfloat16)
        block = basis.T
        for step in range(ITERS):
            part = lax.dot_general(
                block, standard, (((1,), (1,)), ((), ())), preferred_element_type=jnp.float32
            ).astype(jnp.bfloat16)
            scores = total_of(from_all(part, "snp", snake)).astype(jnp.bfloat16)
            local = jnp.dot(scores, standard, preferred_element_type=jnp.float32)
            last = step == ITERS - 1
            block = block_over_samples(local, total, jnp.float32 if last else jnp.bfloat16)
        return scores.T, block.T

    return jax.shard_map(
        per_device,
        mesh=mesh,
        in_specs=(P("samp", "snp"), P("snp", None)),
        out_specs=(P("samp", None), P("snp", None)),
        check_vma=False,
    )
```

```python
import jax
import jax.numpy as jnp
from jax import lax
from jax.sharding import PartitionSpec as P

ITERS = 2
LANES = 128
SUBLANES = 8
HALF = 16


def samp_groups(mesh):
    depth = mesh.shape["samp"] // 4
    at = lambda y, z, c: (y * depth + z) * 2 + c
    four = [(y, c) for y in range(2) for c in range(2)]
    level = [[at(y, z, c) for y, c in four] for z in range(depth)]
    column = [[at(y, z, c) for z in range(depth)] for y, c in four]
    twos = [(z, z + 1) if z < depth // 2 else (z + 1, z) for z in range(0, depth, 2)]
    cell = [[at(y, z, c) for z in two for y, c in four] for two in twos]
    stride = [[at(y, two[k], c) for two in twos] for k in range(2) for y, c in four]
    return level, column, cell, stride


def exchange(blocks, axis, groups):
    return lax.all_to_all(
        blocks, axis, split_axis=0, concat_axis=0, tiled=True, axis_index_groups=groups
    )


def from_all(shard, axis, groups):
    copies = jnp.broadcast_to(shard, (len(groups[0]), *shard.shape))
    return exchange(copies, axis, groups)


def total_of(held):
    return jnp.sum(held.astype(jnp.float32), axis=0)


def solution(mesh):
    level, column, cell, stride = samp_groups(mesh)
    peers = mesh.shape["snp"]
    snake = [[*range(0, peers, 2), *range(peers - 1, 0, -2)]]

    def block_over_samples(local, total, dtype):
        rows, width = local.shape
        members, tiles = len(cell[0]), width // LANES
        cut = local.astype(jnp.bfloat16).reshape(-1, SUBLANES, tiles, LANES)
        cut = cut.transpose(0, 2, 1, 3).reshape(members, -1, SUBLANES // 2, LANES)
        part = total_of(exchange(cut, "samp", cell)).astype(jnp.bfloat16)
        share = (total_of(from_all(part, "samp", stride)) / total).astype(dtype)
        whole = from_all(share, "samp", cell).reshape(-1, tiles, SUBLANES, LANES)
        return whole.transpose(0, 2, 1, 3).reshape(rows, width)

    def per_device(genotype, basis):
        samples, snps = genotype.shape
        total = samples * lax.axis_size("samp")
        observed = genotype < 3
        counts = jnp.sum(jnp.where(observed, genotype + (1 << HALF), 0), axis=0)
        counts = jnp.sum(from_all(counts.reshape(-1, LANES), "samp", level), axis=0)
        held = from_all(counts, "samp", column)
        allele_sum = jnp.sum(held & ((1 << HALF) - 1), axis=0).astype(jnp.float32)
        called = jnp.sum(held >> HALF, axis=0).astype(jnp.float32)
        freq = (allele_sum + 1.0) / (2.0 * called + 2.0)
        scale = 1.0 / jnp.sqrt(2.0 * freq * (1.0 - freq))
        freq, scale = freq.reshape(snps), scale.reshape(snps)
        standard = jnp.where(
            observed, (genotype.astype(jnp.float32) - 2.0 * freq) * scale, 0.0
        ).astype(jnp.bfloat16)
        block = basis.T
        for step in range(ITERS):
            part = lax.dot_general(
                block, standard, (((1,), (1,)), ((), ())), preferred_element_type=jnp.float32
            ).astype(jnp.bfloat16)
            scores = total_of(from_all(part, "snp", snake)).astype(jnp.bfloat16)
            local = jnp.dot(scores, standard, preferred_element_type=jnp.float32)
            last = step == ITERS - 1
            block = block_over_samples(local, total, jnp.float32 if last else jnp.bfloat16)
        return scores.T, block.T

    return jax.shard_map(
        per_device,
        mesh=mesh,
        in_specs=(P("samp", "snp"), P("snp", None)),
        out_specs=(P("samp", None), P("snp", None)),
        check_vma=False,
    )
```

```python
import jax
import jax.numpy as jnp
from jax import lax
from jax.sharding import PartitionSpec as P

ITERS = 2
LANES = 128
SUBLANES = 8
HALF = 16


def samp_groups(mesh):
    depth = mesh.shape["samp"] // 4
    at = lambda y, z, c: (y * depth + z) * 2 + c
    four = [(y, c) for y in range(2) for c in range(2)]
    level = [[at(y, z, c) for y, c in four] for z in range(depth)]
    column = [[at(y, z, c) for z in range(depth)] for y, c in four]
    twos = [(z, z + 1) if z < depth // 2 else (z + 1, z) for z in range(0, depth, 2)]
    cell = [[at(y, z, c) for z in two for y, c in four] for two in twos]
    stride = [[at(y, two[k], c) for two in twos] for k in range(2) for y, c in four]
    return level, column, cell, stride


def exchange(blocks, axis, groups):
    return lax.all_to_all(
        blocks, axis, split_axis=0, concat_axis=0, tiled=True, axis_index_groups=groups
    )


def from_all(shard, axis, groups):
    copies = jnp.broadcast_to(shard, (len(groups[0]), *shard.shape))
    return exchange(copies, axis, groups)


def total_of(held):
    return jnp.sum(held.astype(jnp.float32), axis=0)


def solution(mesh):
    level, column, cell, stride = samp_groups(mesh)
    peers = mesh.shape["snp"]
    snake = [[*range(0, peers, 2), *range(peers - 1, 0, -2)]]

    def block_over_samples(local, total, dtype):
        rows, width = local.shape
        members, tiles = len(cell[0]), width // LANES
        cut = local.astype(jnp.bfloat16).reshape(-1, SUBLANES, tiles, LANES)
        cut = cut.transpose(0, 2, 1, 3).reshape(members, -1, SUBLANES // 2, LANES)
        part = total_of(exchange(cut, "samp", cell)).astype(jnp.bfloat16)
        share = (total_of(from_all(part, "samp", stride)) / total).astype(jnp.bfloat16)
        whole = from_all(share, "samp", cell).astype(dtype).reshape(-1, tiles, SUBLANES, LANES)
        return whole.transpose(0, 2, 1, 3).reshape(rows, width)

    def per_device(genotype, basis):
        samples, snps = genotype.shape
        total = samples * lax.axis_size("samp")
        observed = genotype < 3
        counts = jnp.sum(jnp.where(observed, genotype + (1 << HALF), 0), axis=0)
        counts = jnp.sum(from_all(counts.reshape(-1, LANES), "samp", level), axis=0)
        held = from_all(counts, "samp", column)
        allele_sum = jnp.sum(held & ((1 << HALF) - 1), axis=0).astype(jnp.float32)
        called = jnp.sum(held >> HALF, axis=0).astype(jnp.float32)
        freq = (allele_sum + 1.0) / (2.0 * called + 2.0)
        scale = 1.0 / jnp.sqrt(2.0 * freq * (1.0 - freq))
        freq, scale = freq.reshape(snps), scale.reshape(snps)
        standard = jnp.where(
            observed, (genotype.astype(jnp.float32) - 2.0 * freq) * scale, 0.0
        ).astype(jnp.bfloat16)
        block = basis.T
        for step in range(ITERS):
            part = lax.dot_general(
                block, standard, (((1,), (1,)), ((), ())), preferred_element_type=jnp.float32
            ).astype(jnp.bfloat16)
            scores = total_of(from_all(part, "snp", snake)).astype(jnp.bfloat16)
            local = jnp.dot(scores, standard, preferred_element_type=jnp.float32)
            last = step == ITERS - 1
            block = block_over_samples(local, total, jnp.float32 if last else jnp.bfloat16)
        return scores.T, block.T

    return jax.shard_map(
        per_device,
        mesh=mesh,
        in_specs=(P("samp", "snp"), P("snp", None)),
        out_specs=(P("samp", None), P("snp", None)),
        check_vma=False,
    )
```

```python
import jax
import jax.numpy as jnp
from jax import lax
from jax.sharding import PartitionSpec as P

ITERS = 2
LANES = 128
SUBLANES = 8
HALF = 16


def samp_groups(mesh):
    depth = mesh.shape["samp"] // 4
    at = lambda y, z, c: (y * depth + z) * 2 + c
    four = [(y, c) for y in range(2) for c in range(2)]
    level = [[at(y, z, c) for y, c in four] for z in range(depth)]
    column = [[at(y, z, c) for z in range(depth)] for y, c in four]
    twos = [(z, z + 1) if z < depth // 2 else (z + 1, z) for z in range(0, depth, 2)]
    cell = [[at(y, z, c) for z in two for y, c in four] for two in twos]
    stride = [[at(y, two[k], c) for two in twos] for k in range(2) for y, c in four]
    return level, column, cell, stride


def exchange(blocks, axis, groups):
    return lax.all_to_all(
        blocks, axis, split_axis=0, concat_axis=0, tiled=True, axis_index_groups=groups
    )


def from_all(shard, axis, groups):
    copies = jnp.broadcast_to(shard, (len(groups[0]), *shard.shape))
    return exchange(copies, axis, groups)


def total_of(held):
    return jnp.sum(held.astype(jnp.float32), axis=0)


def solution(mesh):
    level, column, cell, stride = samp_groups(mesh)
    peers = mesh.shape["snp"]
    pairs = [[k, k + 1] for k in range(0, peers, 2)]
    lines = [[*range(k, peers, 2)] for k in range(2)]

    def block_over_samples(local, total, dtype):
        rows, width = local.shape
        members, tiles = len(cell[0]), width // LANES
        cut = local.astype(jnp.bfloat16).reshape(-1, SUBLANES, tiles, LANES)
        cut = cut.transpose(0, 2, 1, 3).reshape(members, -1, SUBLANES // 2, LANES)
        part = total_of(exchange(cut, "samp", cell)).astype(jnp.bfloat16)
        share = (total_of(from_all(part, "samp", stride)) / total).astype(jnp.bfloat16)
        whole = from_all(share, "samp", cell).astype(dtype).reshape(-1, tiles, SUBLANES, LANES)
        return whole.transpose(0, 2, 1, 3).reshape(rows, width)

    def per_device(genotype, basis):
        samples, snps = genotype.shape
        total = samples * lax.axis_size("samp")
        observed = genotype < 3
        counts = jnp.sum(jnp.where(observed, genotype + (1 << HALF), 0), axis=0)
        counts = jnp.sum(from_all(counts.reshape(-1, LANES), "samp", level), axis=0)
        held = from_all(counts, "samp", column)
        allele_sum = jnp.sum(held & ((1 << HALF) - 1), axis=0).astype(jnp.float32)
        called = jnp.sum(held >> HALF, axis=0).astype(jnp.float32)
        freq = (allele_sum + 1.0) / (2.0 * called + 2.0)
        scale = 1.0 / jnp.sqrt(2.0 * freq * (1.0 - freq))
        freq, scale = freq.reshape(snps), scale.reshape(snps)
        standard = jnp.where(
            observed, (genotype.astype(jnp.float32) - 2.0 * freq) * scale, 0.0
        ).astype(jnp.bfloat16)
        block = basis.T
        for step in range(ITERS):
            part = lax.dot_general(
                block, standard, (((1,), (1,)), ((), ())), preferred_element_type=jnp.float32
            ).astype(jnp.bfloat16)
            pair = total_of(lax.all_gather(part, "snp", axis_index_groups=pairs)).astype(jnp.bfloat16)
            scores = total_of(from_all(pair, "snp", lines)).astype(jnp.bfloat16)
            local = jnp.dot(scores, standard, preferred_element_type=jnp.float32)
            last = step == ITERS - 1
            block = block_over_samples(local, total, jnp.float32 if last else jnp.bfloat16)
        return scores.T, block.T

    return jax.shard_map(
        per_device,
        mesh=mesh,
        in_specs=(P("samp", "snp"), P("snp", None)),
        out_specs=(P("samp", None), P("snp", None)),
        check_vma=False,
    )
```
